1024 devices in a mesh: ep: 16 (over z_lo, x), fsdp: 16 (over y, core), dp: 4 (over z_hi).
Axes of the slice: x: 4, y: 8, z: 16 (z_hi: 4, z_lo: 4; z = z_hi * 4 + z_lo), core: 2. Of those that a mesh axis runs over, the one named last changes fastest.
Arguments:
- learner_in: bfloat16 [64, 2048, 1024], P(('ep', 'dp'), 'fsdp'), may hold values from -0.125 to 0.125
- learner_out: bfloat16 [64, 512, 2048], P(('ep', 'dp'), None, 'fsdp'), may hold values from -0.25 to 0.25
- placement: int32 [64], replicated, may hold values from 0 to 63, each once
- hidden: bfloat16 [8192, 2048], P(('ep', 'fsdp', 'dp')), may hold values from -6 to 6
- norm_gain: float32 [2048], replicated, may hold values from 0.1 to 1.9
- expert_ids: int32 [1, 8192, 10], P(None, ('ep', 'fsdp', 'dp')), may hold values from 0 to 63, all different within a row; in each aligned block of 8 rows (0 to 7, 8 to 15, ..., all dimensions but the last counted through in order) at most 2 rows name the same one
- gate_weights: float32 [1, 8192, 10], P(None, ('ep', 'fsdp', 'dp')), may hold values from 0.1 to 0.5
Outputs:
- rollout_in: bfloat16 [64, 2048, 1024], P(('ep', 'dp'))
- rollout_out: bfloat16 [64, 512, 2048], P(('ep', 'dp'))
- final_rows: bfloat16 [8192, 2048], P(('ep', 'fsdp', 'dp'))
The draws below stay inside these ranges and needn't reach their ends.
Inputs may be any that keep to these rules, and one draw needn't show every extreme that they name: `placement`: each expert id appears in exactly one position. `expert_ids`: the 10 ids of a row differ. In each step, no id is named by more than 2 rows of one device; some id reaches 2.
All inputs are finite; a program needn't handle non-finite values.
Results may differ from the reference program's by a relative error of at most 0.0051.
Values may be sent and summed in bfloat16 or wider, within the bound.
A program may use at most 64 MiB of HBM per device.

```python
import math
import jax
import jax.numpy as jnp
import numpy as np
from jax import lax

D = 2048
FF = 512
TOP = 10
QBLOCK = 128
EXPERTS = 64
STEPS = 1
ROWS_DEV = 8
CAP = 2
ROWS = 8192


def steps_of(key, dims, cuts, smallest, largest):
    level = 1.0
    for dim, shards_of in cuts:
        heights = jax.random.uniform(jax.random.fold_in(jax.random.fold_in(key, 6), dim), (shards_of,), jnp.float32, smallest / len(cuts), largest / len(cuts))
        level = level * jnp.repeat(jnp.exp(heights), dims[dim] // shards_of).reshape((-1,) + (1,) * (len(dims) - 1 - dim))
    return level


def deal_out(key, own, number, rows, amount, top, most, slope):
    order = jax.random.permutation(key, amount)
    crowded, usual = portions_of(amount, rows * top, most, slope, True), portions_of(amount, rows * top, most, slope, False)
    places = jnp.arange(amount)

    def named(lengths, turn):
        used = int((lengths > 0).sum())
        fixed = max(1, used // 4)
        passed = fixed + (places - fixed + turn * (used - fixed)) % max(1, amount - fixed)
        return jnp.zeros((amount,), jnp.int32).at[order[jnp.where(places < fixed, places, passed)]].set(jnp.asarray(lengths, jnp.int32))

    lengths = jnp.where(number % 4 == 0, named(crowded, number // 4), named(usual, number - number // 4 - 1))
    mixed = jax.random.permutation(jax.random.fold_in(own, 3), amount)
    source_of, sink = mixed[0:amount // 2 * 2:2], mixed[1:amount // 2 * 2:2]
    margin = jnp.minimum(lengths[source_of] - 1, most - lengths[sink]) // 2
    margin = jnp.where((source_of == order[0]) | (sink == order[0]) | (lengths[sink] == 0), 0, jnp.maximum(margin, 0))
    passed = jax.random.randint(jax.random.fold_in(own, 4), (amount // 2,), 0, 1 << 20) % (margin + 1)
    lengths = lengths.at[source_of].add(-passed).at[sink].add(passed)
    items = jnp.searchsorted(jnp.cumsum(lengths), jnp.arange(rows * top), side="right").astype(jnp.int32)
    listing = items.reshape(top, rows).T
    listing = listing[jax.random.permutation(jax.random.fold_in(own, 1), rows)]
    turn = jax.random.randint(jax.random.fold_in(own, 2), (rows, 1), 0, top)
    return jnp.take_along_axis(listing, (jnp.arange(top)[None, :] + turn) % top, axis=1)


def portions_of(amount, total, limit, skew, full):
    portions = [(1 << 20) // math.isqrt(standing ** skew) + 1 for standing in range(1, amount + 1)]
    largest = limit if full else min(limit, max(-(-total // amount), total * portions[0] // sum(portions)))
    least = 1 if total - largest >= amount - 1 else 0
    counts, surplus = [largest] + [least] * (amount - 1), total - largest - least * (amount - 1)
    while surplus > 0:
        free = [i for i in range(1, amount) if counts[i] < largest] or [i for i in range(1, amount) if counts[i] < limit]
        pool, budget = sum([portions[i] for i in free]), surplus
        for i in free:
            more = min(limit - counts[i], max(1, budget * portions[i] // pool), surplus)
            counts[i] = counts[i] + more
            surplus = surplus - more
    return np.array(counts)


def gaussian(stream_key, extent, spread, limit, pieces=(), held_as=jnp.bfloat16):
    factor_of = steps_of(stream_key, extent, pieces, -0.22, 0.18) if pieces else 1.0
    entries = jax.random.normal(stream_key, extent, jnp.float32) * spread * factor_of
    return jnp.minimum(jnp.maximum(entries, -limit), limit).astype(held_as)


def setup_inputs(seed: int = 0) -> dict:
    streams_of = jax.random.split(jax.random.key(seed), 8)
    learner_in = gaussian(streams_of[0], (EXPERTS, D, 2 * FF), D ** -0.5, 0.125, ((0, 64), (1, 16)))
    learner_out = gaussian(streams_of[1], (EXPERTS, FF, D), FF ** -0.5, 0.25, ((0, 64), (2, 16)))
    placement = jax.random.permutation(streams_of[2], EXPERTS).astype(jnp.int32)
    hidden = gaussian(streams_of[3], (ROWS, D), 1.0, 6.0, ((0, 1024),))
    norm_gain = jnp.clip(1.0 + 0.18 * jax.random.normal(streams_of[4], (D,), jnp.float32), 0.1, 1.9)
    expert_ids_keys = jax.random.split(jax.random.fold_in(streams_of[5], 1), STEPS * ROWS // ROWS_DEV)
    expert_ids_turns = jax.random.permutation(jax.random.fold_in(streams_of[5], 3), STEPS * ROWS // ROWS_DEV)
    expert_ids = jax.vmap(lambda own, number: deal_out(jax.random.fold_in(streams_of[5], 2), own, number, ROWS_DEV, EXPERTS, TOP, CAP, 2))(expert_ids_keys, expert_ids_turns).reshape((STEPS, ROWS, TOP))
    gate_weights = jnp.clip(0.1 + 0.4 * jax.random.uniform(streams_of[6], (STEPS, ROWS, TOP), jnp.float32) ** steps_of(streams_of[6], (STEPS, ROWS, TOP), ((1, 1024),), -0.2, 0.2), 0.1, 0.5)
    return {"learner_in": learner_in, "learner_out": learner_out, "placement": placement, "hidden": hidden, "norm_gain": norm_gain, "expert_ids": expert_ids, "gate_weights": gate_weights}


scale_table = [2.0 ** k for k in range(-40, 16)]
binade_table = [2.0 ** (-k) for k in range(15)]

def block_levels(weights):
    count, height, span = weights.shape
    blocks = weights.astype(jnp.float32).reshape(count, height // QBLOCK, QBLOCK, span // QBLOCK, QBLOCK)
    peak = lax.optimization_barrier(jnp.max(jnp.abs(blocks), axis=(2, 4)))
    candidates = jnp.asarray(scale_table, jnp.float32)
    scales = lax.optimization_barrier(jnp.max(jnp.where(peak[..., None] >= candidates, candidates, candidates[0]), axis=-1)).astype(jnp.bfloat16)
    quotient = blocks / scales.astype(jnp.float32)[:, :, None, :, None]
    magnitude = jnp.abs(quotient)
    binade = jnp.full_like(magnitude, binade_table[-1])
    for threshold in binade_table[:-1]:
        binade = jnp.maximum(binade, jnp.where(magnitude >= threshold, threshold, 0.0))
    rounded = jnp.floor(magnitude / binade * 8.0 + 0.5) * binade * 0.125
    levels = (jnp.sign(quotient) * rounded).astype(jnp.bfloat16)
    return (levels.reshape(count, height, span), scales)

def restore(levels, scales):
    count, height, span = levels.shape
    blocks = levels.reshape(count, height // QBLOCK, QBLOCK, span // QBLOCK, QBLOCK)
    return (blocks * scales[:, :, None, :, None]).reshape(count, height, span)

def expert_apply(packed):
    source, weight_in, weight_out = packed
    project = jnp.dot(source, weight_in, preferred_element_type=jnp.float32)
    inner = (jax.nn.silu(project[:, :FF]) * project[:, FF:]).astype(jnp.bfloat16)
    return jnp.dot(inner, weight_out, preferred_element_type=jnp.float32).astype(jnp.bfloat16)

def reference(learner_in, learner_out, placement, hidden, norm_gain, expert_ids, gate_weights):
    levels_in, scales_in = block_levels(learner_in)
    levels_out, scales_out = block_levels(learner_out)
    levels_in, levels_out = lax.optimization_barrier((levels_in, levels_out))
    rollout_in = restore(levels_in, scales_in)
    rollout_out = restore(levels_out, scales_out)
    column = jnp.arange(EXPERTS, dtype=jnp.int32)
    bound = ROWS // ROWS_DEV * CAP
    state = hidden
    for step in range(STEPS):
        xfull = state.astype(jnp.float32)
        normed = (xfull * lax.rsqrt(lax.optimization_barrier(jnp.mean(xfull * xfull, axis=-1, keepdims=True)) + 1e-06) * norm_gain).astype(jnp.bfloat16)
        slot = placement[expert_ids[step]].astype(jnp.int32).reshape(-1)
        onehot = (slot[:, None] == column[None, :]).astype(jnp.int32)
        rank = lax.optimization_barrier(jnp.sum((jnp.cumsum(onehot, axis=0) - onehot) * onehot, axis=1)).astype(jnp.int32)
        source = jnp.repeat(normed, TOP, axis=0)
        buffer = jnp.zeros((EXPERTS, bound, D), jnp.bfloat16).at[slot, rank].set(source)
        answers = lax.map(expert_apply, (buffer, rollout_in, rollout_out))
        picked = answers[slot, rank].reshape(ROWS, TOP, D)
        combined = lax.optimization_barrier(jnp.sum(gate_weights[step][..., None] * picked.astype(jnp.float32), axis=1))
        state = (xfull + combined).astype(jnp.bfloat16)
    return (rollout_in, rollout_out, state)
```

```python
import jax
import jax.numpy as jnp
from jax import lax
from jax.experimental import pallas as pl
from jax.experimental.pallas import tpu as pltpu
from jax.sharding import PartitionSpec as P

MESH = pl.DeviceIdType.MESH
BF, F32 = jnp.bfloat16, jnp.float32
BLOCK = 128
CHUNKS = ((0, 1, -1), (2, -2), (3, -3, 4))
RELAYS = (3, -3, 6, -6)
HEADS = (0, 3, -3, 6, -6)


def remote(src, dst, send_sem, recv_sem, device):
    return pltpu.make_async_remote_copy(
        src_ref=src,
        dst_ref=dst,
        send_sem=send_sem,
        recv_sem=recv_sem,
        device_id=device,
        device_id_type=MESH,
    )


def dot(a, b):
    return jnp.dot(a, b, preferred_element_type=F32)


def dot_t(a, b):
    return lax.dot_general(a, b, (((1,), (1,)), ((), ())), preferred_element_type=F32)


def iota(shape, dim):
    return lax.broadcasted_iota(jnp.int32, shape, dim)


def block_scales(peaks):
    scales = jnp.full_like(peaks, 2.0**-40)
    for k in range(-39, 16):
        scales = jnp.where(peaks >= 2.0**k, 2.0**k, scales)
    return scales


def quantized(block, scale):
    nudged = block * (1.0 + 2.0**-10)
    spread = nudged * (2.0**20 + 1.0)
    coarse = spread - (spread - nudged)
    anchor = scale * 96.0
    fine = (nudged + anchor) - anchor
    return jnp.where(jnp.abs(block) >= scale * 2.0**-14, coarse, fine).astype(BF)


def fold(a):
    half = a.shape[1] // 2
    return jnp.concatenate([a[:, :half], a[:, half:]], axis=0)


def kernel(
    lin_hbm, lout_hbm, place_hbm, hid_hbm, gain_hbm, ids_hbm, gates_hbm,
    rin, rout, final,
    lin, lout, place, hid, gain, ids, gates,
    bundles, outgoing, arrived, acc, merge,
    ans, back, leaf_out, leaf_in, far_out, far_in, relay_out, relay_in,
    load_sem,
    in_ss, in_rs, out_ss, out_rs, insib_ss, insib_rs, outsib_ss, outsib_rs,
    z_ss, z_rs, x_ss, x_rs, bx_ss, bx_rs, leaf_ss, leaf_rs, far_ss, far_rs, rel_ss, rel_rs,
):
    ep, dp, fs = lax.axis_index("ep"), lax.axis_index("dp"), lax.axis_index("fsdp")
    x, z = ep % 4, dp * 4 + ep // 4
    y, core = fs // 2, fs % 2

    def xz(dx, dz):
        tx, tz = (x + dx + 4) % 4, (z + dz + 16) % 16
        return {"ep": (tz % 4) * 4 + tx, "dp": tz // 4}

    up, down = {"fsdp": (fs + 2) % 16}, {"fsdp": (fs + 14) % 16}
    sibling = {"fsdp": fs + 1 - 2 * core}

    loads = []
    for i, (s, d) in enumerate((
        (lin_hbm, lin), (hid_hbm, hid), (gain_hbm, gain), (ids_hbm, ids),
        (gates_hbm, gates), (place_hbm, place), (lout_hbm, lout),
    )):
        c = pltpu.make_async_copy(s, d, load_sem.at[i])
        c.start()
        loads.append(c)

    barrier = pltpu.get_barrier_semaphore()
    peers = [up, down, sibling] + [xz(d, 0) for d in (1, 2, 3)]
    peers += [xz(0, d) for d in (1, -1, 2, -2, 3, -3, 6, -6)]
    for peer in peers:
        pl.semaphore_signal(barrier, inc=1, device_id=peer, device_id_type=MESH)

    sends = []

    def send(c):
        c.start()
        sends.append(c)
        return c

    def chip_of(distance):
        return (y + distance + 8) % 8

    def in_ref(distance, k, c):
        row = (chip_of(distance) * 2 + c) * 128 + k * 64
        return rin.at[pl.ds(pl.multiple_of(row, 64), 64), :]

    def out_ref(distance, k, c):
        column = (chip_of(distance) * 2 + c) * 128
        return rout.at[pl.ds(k * 256, 256), pl.ds(pl.multiple_of(column, 128), 128)]

    ring = {}

    class Gather:
        def __init__(self, ref, ss, rs, sib_ss, sib_rs):
            self.ref, self.ss, self.rs, self.sib_ss, self.sib_rs = ref, ss, rs, sib_ss, sib_rs
            self.got, self.sib = {}, {}
            self.n = 0
            self.m = 0

        def push(self, step, k, way):
            held = -step if way == 0 else step
            piece = self.ref(held, k, core)
            c = remote(piece, piece, self.ss.at[self.n], self.rs.at[self.n], up if way == 0 else down)
            self.n += 1
            self.got[(step + 1, k, way)] = send(c)

        def share(self, distance, k):
            piece = self.ref(distance, k, core)
            c = remote(piece, piece, self.sib_ss.at[self.m], self.sib_rs.at[self.m], sibling)
            self.m += 1
            self.sib[(distance, k)] = send(c)

        def arrive(self, step, k, way):
            self.got[(step, k, way)].wait_recv()
            if step < 3 or (step == 3 and k == way):
                self.push(step, k, way)
            distance = -step if way == 0 else step
            self.share(4 if step == 4 else distance, k)

        def ready(self, distance):
            for k in (0, 1):
                self.sib[(distance, k)].wait_recv()

    gin = Gather(in_ref, in_ss, in_rs, insib_ss, insib_rs)
    gout = Gather(out_ref, out_ss, out_rs, outsib_ss, outsib_rs)

    loads[0].wait()
    peaks = []
    for b in range(8):
        peaks.append(jnp.max(jnp.abs(lin[:, b * BLOCK:(b + 1) * BLOCK].astype(F32)), axis=0, keepdims=True))
    peak = jnp.max(jnp.concatenate(peaks, axis=0), axis=1, keepdims=True)
    scales = block_scales(jnp.broadcast_to(peak, (8, 128)))
    own_row = fs * 128
    for b in range(8):
        for r in (0, 64):
            block = lin[r:r + 64, b * BLOCK:(b + 1) * BLOCK].astype(F32)
            rin[pl.ds(pl.multiple_of(own_row + r, 64), 64), b * BLOCK:(b + 1) * BLOCK] = quantized(
                block, scales[b:b + 1, :]
            )
    pl.semaphore_wait(barrier, len(peers))
    for k in (0, 1):
        for way in (0, 1):
            gin.push(0, k, way)
    for k in (0, 1):
        gin.share(0, k)

    for c in loads[1:6]:
        c.wait()
    rows = hid[...].astype(F32)
    normed = rows * lax.rsqrt(jnp.mean(rows * rows, axis=-1, keepdims=True) + 1e-06) * gain[...]
    lane8 = iota((8, 128), 1)
    sub8 = iota((8, 128), 0)
    named = jnp.zeros((8, 128), F32)
    weight = jnp.zeros((8, 128), F32)
    idv, gatev = ids[...], gates[...]
    for k in range(idv.shape[1]):
        hit = jnp.broadcast_to(idv[:, k:k + 1], (8, 128)) == lane8
        named = named + jnp.where(hit, 1.0, 0.0)
        weight = weight + jnp.where(hit, jnp.broadcast_to(gatev[:, k:k + 1], (8, 128)), 0.0)
    earlier = jnp.zeros((8, 128), F32)
    for i in range(7):
        earlier = earlier + jnp.where(sub8 > i, jnp.broadcast_to(named[i:i + 1, :], (8, 128)), 0.0)
    code = named * (1.0 + earlier)
    high = weight.astype(BF).astype(F32)
    low = weight - high
    slot = jnp.broadcast_to(place[...], (128, 64))
    column = ((slot & 3) * 4 + (slot >> 4)) * 4 + ((slot >> 2) & 3)
    move = jnp.where(column == (iota((128, 64), 0) & 63), 1.0, 0.0).astype(BF)
    stacked = jnp.concatenate([code, high, low, jnp.zeros((8, 128), F32)], axis=0)[:, :64].astype(BF)
    moved = dot_t(stacked, move)
    info = jnp.concatenate([
        jnp.where(lane8 < 64, moved[0:8], moved[8:16]),
        jnp.where(lane8 < 64, moved[0:8], moved[16:24]),
    ], axis=0)
    bundles[0, :, 0:1024] = fold(normed).astype(BF)
    bundles[0, :, 1024:1152] = info.astype(BF)

    zgot = {}

    def zsend(held, hop, i):
        there = (held - hop) % 16
        zgot[there] = send(remote(
            bundles.at[held % 16], bundles.at[there], z_ss.at[i], z_rs.at[i], xz(0, hop)
        ))

    for i, hop in enumerate((6, -6, 3, -3)):
        zsend(0, hop, i)
    zsend(0, 1, 4)
    zsend(0, -1, 5)

    loads[6].wait()
    peaks = []
    for b in range(4):
        peaks.append(jnp.max(jnp.abs(lout[b * BLOCK:(b + 1) * BLOCK, :].astype(F32)), axis=0, keepdims=True))
    peak = jnp.max(jnp.concatenate(peaks + peaks, axis=0), axis=1, keepdims=True)
    scales = block_scales(jnp.broadcast_to(peak, (8, 128)))
    own_column = pl.ds(pl.multiple_of(fs * 128, 128), 128)
    for b in range(4):
        for r in (0, 64):
            here = slice(b * BLOCK + r, b * BLOCK + r + 64)
            rout[here, own_column] = quantized(lout[here, :].astype(F32), scales[b:b + 1, :])
    for k in (0, 1):
        gout.share(0, k)

    gin.arrive(1, 0, 0)
    gin.arrive(1, 0, 1)
    number = 6
    for held in (3, -3, 6, -6):
        zgot[held % 16].wait_recv()
        for hop in (1, -1):
            zsend(held, hop, number)
            number += 1
        if held == 6:
            zsend(held, -2, number)
            number += 1
    gin.arrive(1, 1, 0)
    gin.arrive(1, 1, 1)
    gin.arrive(2, 0, 0)
    gin.arrive(2, 0, 1)

    for offset in range(1, 16):
        if offset not in (3, 13, 6, 10):
            zgot[offset].wait_recv()
    every = bundles[...].reshape(256, 1152)
    table, held_rows = every[:, 1024:], every[:, :1024]
    line, lane = iota((128, 128), 0), iota((128, 128), 1)
    target = 4 * z + ((x + (line >> 5)) & 3)
    pick = jnp.where(lane == target, 1.0, 0.0).astype(BF)
    pick_gate = jnp.where(lane == target + 64, 1.0, 0.0).astype(BF)
    line, lane = iota((128, 256), 0), iota((128, 256), 1)
    same = ((line >> 1) & 15) == (lane >> 4)
    chosen = jnp.where(same, dot_t(pick, table), 0.0) == ((line & 1) + 1).astype(F32)
    left = jnp.where(chosen, jnp.where((lane & 8) == 0, 1.0, 0.0), 0.0).astype(BF)
    right = jnp.where(chosen, jnp.where((lane & 8) == 0, 0.0, 1.0), 0.0).astype(BF)
    outgoing[:, 0:1024] = dot(left, held_rows).astype(BF)
    outgoing[:, 1024:2048] = dot(right, held_rows).astype(BF)
    xgot = []
    for dx in (2, 1, 3):
        block = pl.ds(dx * 32, 32)
        xgot.append(send(remote(
            outgoing.at[block, :], arrived.at[block, :], x_ss.at[dx], x_rs.at[dx], xz(dx, 0)
        )))
    arrived[0:32, :] = outgoing[0:32, :]
    line, lane = iota((256, 128), 0), iota((256, 128), 1)
    same = ((lane >> 1) & 15) == (line >> 4)
    chosen = jnp.where(same, dot_t(table, pick), 0.0) == ((lane & 1) + 1).astype(F32)
    merge[...] = jnp.where(chosen, dot_t(table, pick_gate), 0.0).astype(BF)

    gin.arrive(2, 1, 0)
    gin.arrive(2, 1, 1)
    gin.arrive(3, 0, 0)
    gin.arrive(3, 0, 1)
    for c in xgot:
        c.wait_recv()

    def project(distance, first=False):
        gin.ready(distance)
        start = pl.multiple_of(chip_of(distance) * 256, 256)
        part = dot(arrived[:, pl.ds(start, 256)], rin[pl.ds(start, 256), :])
        if first:
            acc[...] = part
        else:
            acc[...] += part

    project(0, True)
    gin.arrive(3, 1, 0)
    gin.arrive(3, 1, 1)
    for k in (0, 1):
        for way in (0, 1):
            gout.push(0, k, way)
    for distance in (1, -1, 2, -2, 3, -3):
        project(distance)
    gin.arrive(4, 0, 0)
    gin.arrive(4, 1, 1)
    project(4)
    gate, lift = acc[:, 0:512], acc[:, 512:1024]
    units = (gate / (1.0 + jnp.exp(-gate)) * lift).astype(BF)

    starts, total = [], 0
    for chunk in CHUNKS:
        starts.append(total)
        total += 256 * len(chunk)
    bgot, lgot, rgot, kept = {}, {}, {}, {}

    def answer(n):
        chunk, start = CHUNKS[n], starts[n]
        for m, distance in enumerate(chunk):
            gout.ready(distance)
            column = pl.multiple_of(chip_of(distance) * 256, 256)
            ans[:, start + 256 * m:start + 256 * (m + 1)] = dot(
                units, rout[:, pl.ds(column, 256)]
            ).astype(BF)
        columns = pl.ds(start, 256 * len(chunk))
        bgot[n] = []
        for dx in (2, 1, 3):
            block = pl.ds(dx * 32, 32)
            bgot[n].append(send(remote(
                ans.at[block, columns], back.at[block, columns],
                bx_ss.at[3 * n + dx - 1], bx_rs.at[3 * n + dx - 1], xz(-dx, 0),
            )))
        back[0:32, start:start + 256 * len(chunk)] = ans[0:32, start:start + 256 * len(chunk)]

    def spread(n):
        start, width = starts[n], 256 * len(CHUNKS[n])
        for c in bgot[n]:
            c.wait_recv()
        sums = dot(merge[...], back[:, start:start + width])

        def part(offset):
            at = (offset % 16) * 16
            return fold(sums[at:at + 8] + sums[at + 8:at + 16])

        half = pl.ds(start // 2, width // 2)
        where = slice(start // 2, start // 2 + width // 2)
        lgot[n] = []
        for j, hop in enumerate((1, -1)):
            for i, head in enumerate(HEADS):
                leaf_out[j, 16 * i:16 * i + 16, where] = part(head + hop).astype(BF)
            lgot[n].append(send(remote(
                leaf_out.at[j, :, half], leaf_in.at[j, :, half],
                leaf_ss.at[2 * n + j], leaf_rs.at[2 * n + j], xz(0, hop),
            )))
        far_out[:, where] = part(8).astype(BF)
        lgot[n].append(send(remote(
            far_out.at[:, half], far_in.at[:, half], far_ss.at[n], far_rs.at[n], xz(0, 2)
        )))
        kept[n] = [part(head) for head in HEADS]

    def relay(n):
        start, width = starts[n], 256 * len(CHUNKS[n])
        half = pl.ds(start // 2, width // 2)
        where = slice(start // 2, start // 2 + width // 2)
        for c in lgot[n]:
            c.wait_recv()
        rgot[n] = []
        for i, head in reversed(list(enumerate(HEADS))):
            spot = slice(16 * i, 16 * i + 16)
            value = kept[n][i] + leaf_in[0, spot, where].astype(F32) + leaf_in[1, spot, where].astype(F32)
            if head == 6:
                value = value + far_in[:, where].astype(F32)
            if head == 0:
                kept[n] = value
            else:
                relay_out[i - 1, :, where] = value.astype(BF)
                rgot[n].append(send(remote(
                    relay_out.at[i - 1, :, half], relay_in.at[i - 1, :, half],
                    rel_ss.at[4 * n + i - 1], rel_rs.at[4 * n + i - 1], xz(0, head),
                )))

    def finish(n):
        start, width = starts[n], 256 * len(CHUNKS[n])
        where = slice(start // 2, start // 2 + width // 2)
        for c in rgot[n]:
            c.wait_recv()
        value = kept[n]
        for i in range(4):
            value = value + relay_in[i, :, where].astype(F32)
        whole = jnp.concatenate([value[0:8], value[8:16]], axis=1)
        for m, distance in enumerate(CHUNKS[n]):
            column = pl.ds(pl.multiple_of(chip_of(distance) * 256, 256), 256)
            final[:, column] = (
                hid[:, column].astype(F32) + whole[:, 256 * m:256 * (m + 1)]
            ).astype(BF)

    for k in (0, 1):
        for way in (0, 1):
            gout.arrive(1, k, way)
    answer(0)
    for k in (0, 1):
        for way in (0, 1):
            gout.arrive(2, k, way)
    answer(1)
    spread(0)
    for k in (0, 1):
        for way in (0, 1):
            gout.arrive(3, k, way)
    relay(0)
    spread(1)
    gout.arrive(4, 0, 0)
    gout.arrive(4, 1, 1)
    answer(2)
    relay(1)
    spread(2)
    finish(0)
    finish(1)
    relay(2)
    finish(2)
    for c in sends:
        c.wait_send()


def per_device(learner_in, learner_out, placement, hidden, norm_gain, expert_ids, gate_weights):
    dma = pltpu.SemaphoreType.DMA
    vmem = pltpu.VMEM
    chunks = len(CHUNKS)
    rin, rout, final = pl.pallas_call(
        kernel,
        out_shape=(
            jax.ShapeDtypeStruct((2048, 1024), BF),
            jax.ShapeDtypeStruct((512, 2048), BF),
            jax.ShapeDtypeStruct((8, 2048), BF),
        ),
        in_specs=[pl.BlockSpec(memory_space=pl.ANY)] * 7,
        out_specs=[pl.BlockSpec(memory_space=pltpu.VMEM)] * 3,
        scratch_shapes=[
            vmem((128, 1024), BF), vmem((512, 128), BF), vmem((1, 64), jnp.int32), vmem((8, 2048), BF),
            vmem((1, 2048), F32), vmem((8, 10), jnp.int32), vmem((8, 10), F32),
            vmem((16, 16, 1152), BF), vmem((128, 2048), BF), vmem((128, 2048), BF),
            vmem((128, 1024), F32), vmem((256, 128), BF),
            vmem((128, 2048), BF), vmem((128, 2048), BF),
            vmem((2, 80, 1024), BF), vmem((2, 80, 1024), BF), vmem((16, 1024), BF), vmem((16, 1024), BF),
            vmem((4, 16, 1024), BF), vmem((4, 16, 1024), BF),
            dma((7,)),
            dma((14,)), dma((14,)), dma((14,)), dma((14,)),
            dma((16,)), dma((16,)), dma((16,)), dma((16,)),
            dma((16,)), dma((16,)), dma((4,)), dma((4,)),
            dma((3 * chunks,)), dma((3 * chunks,)), dma((2 * chunks,)), dma((2 * chunks,)),
            dma((chunks,)), dma((chunks,)), dma((4 * chunks,)), dma((4 * chunks,)),
        ],
        compiler_params=pltpu.CompilerParams(
            collective_id=0, has_side_effects=True, vmem_limit_bytes=40 * 2**20
        ),
    )(
        learner_in.reshape(128, 1024), learner_out.reshape(512, 128), placement.reshape(1, 64), hidden,
        norm_gain.reshape(1, 2048), expert_ids.reshape(8, 10), gate_weights.reshape(8, 10),
    )
    return rin[None], rout[None], final


def solution(mesh):
    in_specs = (
        P(("ep", "dp"), "fsdp", None),
        P(("ep", "dp"), None, "fsdp"),
        P(),
        P(("ep", "fsdp", "dp"), None),
        P(),
        P(None, ("ep", "fsdp", "dp"), None),
        P(None, ("ep", "fsdp", "dp"), None),
    )
    out_specs = (
        P(("ep", "dp"), None, None),
        P(("ep", "dp"), None, None),
        P(("ep", "fsdp", "dp"), None),
    )
    return jax.shard_map(
        per_device, mesh=mesh, in_specs=in_specs, out_specs=out_specs, check_vma=False
    )
```

```python
import jax
import jax.numpy as jnp
from jax import lax
from jax.experimental import pallas as pl
from jax.experimental.pallas import tpu as pltpu
from jax.sharding import PartitionSpec as P

MESH = pl.DeviceIdType.MESH
BF, F32 = jnp.bfloat16, jnp.float32
BLOCK = 128
CHUNKS = ((0, 1, -1), (2, -2), (3, -3), (4,))
STARTS = (0, 768, 1280, 1792)
HEADS = (0, 3, -3, 6, -6)
OFFSETS = (0, 1, -1, 2, -2, 3, -3, 4, -4, 5, -5, 6, -6, 7, -7, 8)


def remote(src, dst, send_sem, recv_sem, device):
    return pltpu.make_async_remote_copy(
        src_ref=src,
        dst_ref=dst,
        send_sem=send_sem,
        recv_sem=recv_sem,
        device_id=device,
        device_id_type=MESH,
    )


def dot(a, b):
    return jnp.dot(a, b, preferred_element_type=F32)


def dot_t(a, b):
    return lax.dot_general(a, b, (((1,), (1,)), ((), ())), preferred_element_type=F32)


def iota(shape, dim):
    return lax.broadcasted_iota(jnp.int32, shape, dim)


def block_scales(peaks):
    scales = jnp.full_like(peaks, 2.0**-40)
    for k in range(-39, 16):
        scales = jnp.where(peaks >= 2.0**k, 2.0**k, scales)
    return scales


def quantized(block, scale):
    nudged = block * (1.0 + 2.0**-10)
    spread = nudged * (2.0**20 + 1.0)
    coarse = spread - (spread - nudged)
    anchor = scale * 96.0
    fine = (nudged + anchor) - anchor
    return jnp.where(jnp.abs(block) >= scale * 2.0**-14, coarse, fine).astype(BF)


def place_of(distance):
    return OFFSETS.index((distance + 7) % 16 - 7)


def fold(a):
    half = a.shape[1] // 2
    return jnp.concatenate([a[:, :half], a[:, half:]], axis=0)


def kernel(
    lin_hbm, lout_hbm, place_hbm, hid_hbm, gain_hbm, ids_hbm, gates_hbm,
    rin, rout, final,
    lin, lout, place, hid, gain, ids, gates,
    bundles, outgoing, arrived, acc, merge,
    ans, back, leaf_out, leaf_in, far_out, far_in, relay_out, relay_in, last_out, last_in,
    load_sem,
    in_ss, in_rs, out_ss, out_rs, insib_ss, insib_rs, outsib_ss, outsib_rs,
    z_ss, z_rs, x_ss, x_rs, bx_ss, bx_rs, leaf_ss, leaf_rs, far_ss, far_rs, rel_ss, rel_rs, last_ss, last_rs,
):
    ep, dp, fs = lax.axis_index("ep"), lax.axis_index("dp"), lax.axis_index("fsdp")
    x, z = ep % 4, dp * 4 + ep // 4
    y, core = fs // 2, fs % 2

    def xz(dx, dz):
        tx, tz = (x + dx + 4) % 4, (z + dz + 16) % 16
        return {"ep": (tz % 4) * 4 + tx, "dp": tz // 4}

    up, down = {"fsdp": (fs + 2) % 16}, {"fsdp": (fs + 14) % 16}
    sibling = {"fsdp": fs + 1 - 2 * core}

    loads = []
    for i, (s, d) in enumerate((
        (lin_hbm, lin), (hid_hbm, hid), (gain_hbm, gain), (ids_hbm, ids),
        (gates_hbm, gates), (place_hbm, place), (lout_hbm, lout),
    )):
        c = pltpu.make_async_copy(s, d, load_sem.at[i])
        c.start()
        loads.append(c)

    barrier = pltpu.get_barrier_semaphore()
    peers = [up, down, sibling] + [xz(d, 0) for d in (1, 2, 3)]
    peers += [xz(0, d) for d in OFFSETS[1:]]
    for peer in peers:
        pl.semaphore_signal(barrier, inc=1, device_id=peer, device_id_type=MESH)

    sends = []

    def send(c):
        c.start()
        sends.append(c)
        return c

    def chip_of(distance):
        return (y + distance + 8) % 8

    def in_ref(distance, k, c):
        row = (chip_of(distance) * 2 + c) * 128 + k * 64
        return rin.at[pl.ds(pl.multiple_of(row, 64), 64), :]

    def out_ref(distance, k, c):
        column = (chip_of(distance) * 2 + c) * 128
        return rout.at[pl.ds(k * 128, 128), pl.ds(pl.multiple_of(column, 128), 128)]

    ring = {}

    class Gather:
        def __init__(self, ref, pieces, ss, rs, sib_ss, sib_rs):
            self.ref, self.pieces = ref, pieces
            self.ss, self.rs, self.sib_ss, self.sib_rs = ss, rs, sib_ss, sib_rs
            self.got, self.sib = {}, {}
            self.n = 0
            self.m = 0

        def push(self, step, k, way):
            held = -step if way == 0 else step
            piece = self.ref(held, k, core)
            c = remote(piece, piece, self.ss.at[self.n], self.rs.at[self.n], up if way == 0 else down)
            self.n += 1
            self.got[(step + 1, k, way)] = send(c)

        def share(self, distance, k):
            piece = self.ref(distance, k, core)
            c = remote(piece, piece, self.sib_ss.at[self.m], self.sib_rs.at[self.m], sibling)
            self.m += 1
            self.sib[(distance, k)] = send(c)

        def begin(self):
            for k in range(self.pieces):
                for way in (0, 1):
                    self.push(0, k, way)

        def begin_share(self):
            for k in range(self.pieces):
                self.share(0, k)

        def arrive(self, step, k):
            ways = (0, 1) if step < 4 else (int(k >= self.pieces // 2),)
            for way in ways:
                self.got[(step, k, way)].wait_recv()
                if step < 3 or (step == 3 and way == int(k >= self.pieces // 2)):
                    self.push(step, k, way)
            for way in ways:
                self.share(4 if step == 4 else (-step if way == 0 else step), k)

        def ready(self, distance):
            for k in range(self.pieces):
                self.sib[(distance, k)].wait_recv()

    gin = Gather(in_ref, 2, in_ss, in_rs, insib_ss, insib_rs)
    gout = Gather(out_ref, 4, out_ss, out_rs, outsib_ss, outsib_rs)

    loads[0].wait()
    peaks = []
    for b in range(8):
        peaks.append(jnp.max(jnp.abs(lin[:, b * BLOCK:(b + 1) * BLOCK].astype(F32)), axis=0, keepdims=True))
    peak = jnp.max(jnp.concatenate(peaks, axis=0), axis=1, keepdims=True)
    scales = block_scales(jnp.broadcast_to(peak, (8, 128)))
    own_row = fs * 128
    for b in range(8):
        for r in (0, 64):
            block = lin[r:r + 64, b * BLOCK:(b + 1) * BLOCK].astype(F32)
            rin[pl.ds(pl.multiple_of(own_row + r, 64), 64), b * BLOCK:(b + 1) * BLOCK] = quantized(
                block, scales[b:b + 1, :]
            )
    pl.semaphore_wait(barrier, len(peers))
    gin.begin()

    for c in loads[1:6]:
        c.wait()
    rows = hid[...].astype(F32)
    normed = rows * lax.rsqrt(jnp.mean(rows * rows, axis=-1, keepdims=True) + 1e-06) * gain[...]
    lane8 = iota((8, 128), 1)
    sub8 = iota((8, 128), 0)
    named = jnp.zeros((8, 128), F32)
    weight = jnp.zeros((8, 128), F32)
    idv, gatev = ids[...], gates[...]
    for k in range(idv.shape[1]):
        hit = jnp.broadcast_to(idv[:, k:k + 1], (8, 128)) == lane8
        named = named + jnp.where(hit, 1.0, 0.0)
        weight = weight + jnp.where(hit, jnp.broadcast_to(gatev[:, k:k + 1], (8, 128)), 0.0)
    earlier = jnp.zeros((8, 128), F32)
    for i in range(7):
        earlier = earlier + jnp.where(sub8 > i, jnp.broadcast_to(named[i:i + 1, :], (8, 128)), 0.0)
    code = named * (1.0 + earlier)
    high = weight.astype(BF).astype(F32)
    low = weight - high
    slot = jnp.broadcast_to(place[...], (128, 64))
    column = ((slot & 3) * 4 + (slot >> 4)) * 4 + ((slot >> 2) & 3)
    move = jnp.where(column == (iota((128, 64), 0) & 63), 1.0, 0.0).astype(BF)
    stacked = jnp.concatenate([code, high, low, jnp.zeros((8, 128), F32)], axis=0)[:, :64].astype(BF)
    moved = dot_t(stacked, move)
    info = jnp.concatenate([
        jnp.where(lane8 < 64, moved[0:8], moved[8:16]),
        jnp.where(lane8 < 64, moved[0:8], moved[16:24]),
    ], axis=0)
    bundles[0, :, 0:1024] = fold(normed).astype(BF)
    bundles[0, :, 1024:1152] = info.astype(BF)

    zgot = {}

    def zsend(held, hop):
        here, there = place_of(held), place_of(held - hop)
        zgot[there] = send(remote(
            bundles.at[here], bundles.at[there], z_ss.at[there], z_rs.at[there], xz(0, hop)
        ))

    for hop in (3, -3, 1, -1, 6, -6):
        zsend(0, hop)
    gin.begin_share()

    loads[6].wait()
    peaks = []
    for b in range(4):
        peaks.append(jnp.max(jnp.abs(lout[b * BLOCK:(b + 1) * BLOCK, :].astype(F32)), axis=0, keepdims=True))
    peak = jnp.max(jnp.concatenate(peaks + peaks, axis=0), axis=1, keepdims=True)
    scales = block_scales(jnp.broadcast_to(peak, (8, 128)))
    own_column = pl.ds(pl.multiple_of(fs * 128, 128), 128)
    for b in range(4):
        for r in (0, 64):
            here = slice(b * BLOCK + r, b * BLOCK + r + 64)
            rout[here, own_column] = quantized(lout[here, :].astype(F32), scales[b:b + 1, :])
    gout.begin_share()

    def relay_rows(held):
        zgot[place_of(held)].wait_recv()
        for hop in (1, -1):
            zsend(held, hop)
        if held == 6:
            zsend(held, -2)

    xgot = []
    line, lane = iota((64, 128), 0), iota((64, 128), 1)
    target = 4 * z + ((x + (line >> 4)) & 3)
    pick = jnp.where(lane == target, 1.0, 0.0).astype(BF)
    pick_gate = jnp.where(lane == target + 64, 1.0, 0.0).astype(BF)

    def select(half):
        for distance in OFFSETS[8 * half:8 * half + 8]:
            if distance not in HEADS:
                zgot[place_of(distance)].wait_recv()
        every = bundles[8 * half:8 * half + 8].reshape(128, 1152)
        table, held_rows = every[:, 1024:], every[:, :1024]
        line, lane = iota((64, 128), 0), iota((64, 128), 1)
        same = ((line >> 1) & 7) == (lane >> 4)
        chosen = jnp.where(same, dot_t(pick, table), 0.0) == ((line & 1) + 1).astype(F32)
        left = jnp.where(chosen, jnp.where((lane & 8) == 0, 1.0, 0.0), 0.0).astype(BF)
        right = jnp.where(chosen, jnp.where((lane & 8) == 0, 0.0, 1.0), 0.0).astype(BF)
        rows_of = slice(64 * half, 64 * half + 64)
        outgoing[rows_of, 0:1024] = dot(left, held_rows).astype(BF)
        outgoing[rows_of, 1024:2048] = dot(right, held_rows).astype(BF)
        for dx in (2, 1, 3):
            block = pl.ds(64 * half + dx * 16, 16)
            xgot.append(send(remote(
                outgoing.at[block, :], arrived.at[block, :],
                x_ss.at[4 * half + dx], x_rs.at[4 * half + dx], xz(dx, 0),
            )))
        arrived[64 * half:64 * half + 16, :] = outgoing[64 * half:64 * half + 16, :]
        line, lane = iota((128, 64), 0), iota((128, 64), 1)
        same = ((lane >> 1) & 7) == (line >> 4)
        chosen = jnp.where(same, dot_t(table, pick), 0.0) == ((lane & 1) + 1).astype(F32)
        merge[128 * half:128 * half + 128, :] = jnp.where(chosen, dot_t(table, pick_gate), 0.0).astype(BF)

    gin.arrive(1, 0)
    relay_rows(3)
    relay_rows(-3)
    gin.arrive(1, 1)
    relay_rows(6)
    relay_rows(-6)
    gin.arrive(2, 0)
    select(0)
    gin.arrive(2, 1)
    gin.arrive(3, 0)
    select(1)
    gin.arrive(3, 1)
    gout.begin()
    gin.arrive(4, 0)
    gin.arrive(4, 1)
    for c in xgot:
        c.wait_recv()

    def project(distance, first=False):
        gin.ready(distance)
        start = pl.multiple_of(chip_of(distance) * 256, 256)
        part = dot(arrived[:, pl.ds(start, 256)], rin[pl.ds(start, 256), :])
        if first:
            acc[...] = part
        else:
            acc[...] += part

    project(0, True)
    for distance in (1, -1, 2, -2):
        project(distance)
    gout.arrive(1, 0)
    gout.arrive(1, 1)
    for distance in (3, -3):
        project(distance)
    gout.arrive(1, 2)
    gout.arrive(1, 3)
    project(4)
    gate, lift = acc[:, 0:512], acc[:, 512:1024]
    units = (gate / (1.0 + jnp.exp(-gate)) * lift).astype(BF)

    bgot, lgot, rgot, kept = {}, {}, {}, {}

    def answer(n):
        chunk, start = CHUNKS[n], STARTS[n]
        for m, distance in enumerate(chunk):
            gout.ready(distance)
            column = pl.multiple_of(chip_of(distance) * 256, 256)
            ans[:, :, start + 256 * m:start + 256 * (m + 1)] = dot(
                units, rout[:, pl.ds(column, 256)]
            ).astype(BF).reshape(2, 64, 256)
        columns = pl.ds(start, 256 * len(chunk))
        bgot[n] = []
        for dx in (2, 1, 3):
            block = pl.ds(dx * 16, 16)
            bgot[n].append(send(remote(
                ans.at[:, block, columns], back.at[:, block, columns],
                bx_ss.at[3 * n + dx - 1], bx_rs.at[3 * n + dx - 1], xz(-dx, 0),
            )))
        back[:, 0:16, start:start + 256 * len(chunk)] = ans[:, 0:16, start:start + 256 * len(chunk)]

    def spread(n):
        start, width = STARTS[n], 256 * len(CHUNKS[n])
        for c in bgot[n]:
            c.wait_recv()
        sums = [dot(merge[128 * b:128 * b + 128, :], back[b, :, start:start + width]) for b in (0, 1)]

        def part(distance):
            half, at = place_of(distance) // 8, place_of(distance) % 8 * 16
            return fold(sums[half][at:at + 8] + sums[half][at + 8:at + 16])

        if n == 3:
            lgot[n] = []
            for i in range(15, 0, -1):
                last_out[i] = part(OFFSETS[i]).astype(BF)
                lgot[n].append(send(remote(
                    last_out.at[i], last_in.at[i], last_ss.at[i], last_rs.at[i], xz(0, OFFSETS[i])
                )))
            kept[n] = part(0)
            return

        half = pl.ds(start // 2, width // 2)
        where = slice(start // 2, start // 2 + width // 2)
        lgot[n] = []
        for j, hop in enumerate((1, -1)):
            for i, head in enumerate(HEADS):
                leaf_out[j, 16 * i:16 * i + 16, where] = part(head + hop).astype(BF)
            lgot[n].append(send(remote(
                leaf_out.at[j, :, half], leaf_in.at[j, :, half],
                leaf_ss.at[2 * n + j], leaf_rs.at[2 * n + j], xz(0, hop),
            )))
        far_out[:, where] = part(8).astype(BF)
        lgot[n].append(send(remote(
            far_out.at[:, half], far_in.at[:, half], far_ss.at[n], far_rs.at[n], xz(0, 2)
        )))
        kept[n] = [part(head) for head in HEADS]

    def relay(n):
        start, width = STARTS[n], 256 * len(CHUNKS[n])
        half = pl.ds(start // 2, width // 2)
        where = slice(start // 2, start // 2 + width // 2)
        for c in lgot[n]:
            c.wait_recv()
        rgot[n] = []
        for i, head in reversed(list(enumerate(HEADS))):
            spot = slice(16 * i, 16 * i + 16)
            value = kept[n][i] + leaf_in[0, spot, where].astype(F32) + leaf_in[1, spot, where].astype(F32)
            if head == 6:
                value = value + far_in[:, where].astype(F32)
            if head == 0:
                kept[n] = value
            else:
                relay_out[i - 1, :, where] = value.astype(BF)
                rgot[n].append(send(remote(
                    relay_out.at[i - 1, :, half], relay_in.at[i - 1, :, half],
                    rel_ss.at[4 * n + i - 1], rel_rs.at[4 * n + i - 1], xz(0, head),
                )))

    def finish(n):
        start, width = STARTS[n], 256 * len(CHUNKS[n])
        where = slice(start // 2, start // 2 + width // 2)
        for c in lgot[n] if n == 3 else rgot[n]:
            c.wait_recv()
        value = kept[n]
        for got in [last_in[i] for i in range(1, 16)] if n == 3 else [relay_in[i, :, where] for i in range(4)]:
            value = value + got.astype(F32)
        whole = jnp.concatenate([value[0:8], value[8:16]], axis=1)
        for m, distance in enumerate(CHUNKS[n]):
            column = pl.ds(pl.multiple_of(chip_of(distance) * 256, 256), 256)
            final[:, column] = (
                hid[:, column].astype(F32) + whole[:, 256 * m:256 * (m + 1)]
            ).astype(BF)

    gout.arrive(2, 0)
    answer(0)
    gout.arrive(2, 1)
    gout.arrive(2, 2)
    gout.arrive(2, 3)
    gout.arrive(3, 0)
    answer(1)
    gout.arrive(3, 1)
    spread(0)
    gout.arrive(3, 2)
    gout.arrive(3, 3)
    answer(2)
    for k in range(4):
        gout.arrive(4, k)
    spread(1)
    relay(0)
    answer(3)
    spread(2)
    spread(3)
    relay(1)
    relay(2)
    finish(0)
    finish(1)
    finish(2)
    finish(3)
    for c in sends:
        c.wait_send()


def per_device(learner_in, learner_out, placement, hidden, norm_gain, expert_ids, gate_weights):
    dma = pltpu.SemaphoreType.DMA
    vmem = pltpu.VMEM
    chunks = len(CHUNKS)
    rin, rout, final = pl.pallas_call(
        kernel,
        out_shape=(
            jax.ShapeDtypeStruct((2048, 1024), BF),
            jax.ShapeDtypeStruct((512, 2048), BF),
            jax.ShapeDtypeStruct((8, 2048), BF),
        ),
        in_specs=[pl.BlockSpec(memory_space=pl.ANY)] * 7,
        out_specs=[pl.BlockSpec(memory_space=pltpu.VMEM)] * 3,
        scratch_shapes=[
            vmem((128, 1024), BF), vmem((512, 128), BF), vmem((1, 64), jnp.int32), vmem((8, 2048), BF),
            vmem((1, 2048), F32), vmem((8, 10), jnp.int32), vmem((8, 10), F32),
            vmem((16, 16, 1152), BF), vmem((128, 2048), BF), vmem((128, 2048), BF),
            vmem((128, 1024), F32), vmem((256, 64), BF),
            vmem((2, 64, 2048), BF), vmem((2, 64, 2048), BF),
            vmem((2, 80, 1024), BF), vmem((2, 80, 1024), BF), vmem((16, 1024), BF), vmem((16, 1024), BF),
            vmem((4, 16, 1024), BF), vmem((4, 16, 1024), BF),
            vmem((16, 16, 128), BF), vmem((16, 16, 128), BF),
            dma((7,)),
            dma((14,)), dma((14,)), dma((28,)), dma((28,)),
            dma((16,)), dma((16,)), dma((32,)), dma((32,)),
            dma((16,)), dma((16,)), dma((8,)), dma((8,)),
            dma((3 * chunks,)), dma((3 * chunks,)), dma((2 * chunks,)), dma((2 * chunks,)),
            dma((chunks,)), dma((chunks,)), dma((4 * chunks,)), dma((4 * chunks,)), dma((16,)), dma((16,)),
        ],
        compiler_params=pltpu.CompilerParams(
            collective_id=0, has_side_effects=True, vmem_limit_bytes=40 * 2**20
        ),
    )(
        *[pltpu.with_memory_space_constraint(a, pltpu.HBM) for a in (learner_in.reshape(128, 1024), learner_out.reshape(512, 128), placement.reshape(1, 64), hidden,
        norm_gain.reshape(1, 2048), expert_ids.reshape(8, 10), gate_weights.reshape(8, 10))]
    )
    return rin[None], rout[None], final


def solution(mesh):
    in_specs = (
        P(("ep", "dp"), "fsdp", None),
        P(("ep", "dp"), None, "fsdp"),
        P(),
        P(("ep", "fsdp", "dp"), None),
        P(),
        P(None, ("ep", "fsdp", "dp"), None),
        P(None, ("ep", "fsdp", "dp"), None),
    )
    out_specs = (
        P(("ep", "dp"), None, None),
        P(("ep", "dp"), None, None),
        P(("ep", "fsdp", "dp"), None),
    )
    return jax.shard_map(
        per_device, mesh=mesh, in_specs=in_specs, out_specs=out_specs, check_vma=False
    )
```
